32 devices in a mesh: gx: 4 (over y, x), gy: 8 (over z, core).
Axes of the slice: x: 2, y: 2, z: 4, core: 2. Of those that a mesh axis runs over, the one named last changes fastest.
Arguments:
- tracer: float32 [6, 1024, 512], P(None, 'gy', 'gx'), may hold values from -6 to 6
- courant: float32 [2, 2, 1024, 512], P(None, None, 'gy', 'gx'), may hold values from 0.05 to 0.95
- displacement: int32 [2, 2, 8, 4], P(None, None, 'gy', 'gx'), may hold values from -16 to 16, as said below
- cotangent: float32 [6, 1024, 512], P(None, 'gy', 'gx'), may hold values from -6 to 6
Outputs:
- tracer_grad: float32 [6, 1024, 512], P(None, 'gy', 'gx')
- courant_grad: float32 [2, 2, 1024, 512], P(None, None, 'gy', 'gx')
The draws below stay inside these ranges and needn't reach their ends.
Inputs may be any that keep to these rules, and one draw needn't show every extreme that they name: `displacement`: in every draw each of the two steps has a block with row and column offsets 16 and a block with row and column offsets -16.
All inputs are finite; a program needn't handle non-finite values.
Results may differ from the reference program's by a relative error of at most 0.0001.
Values sent between devices are 32-bit elements; how exact they have to be, the bound alone decides.
A program may use at most 64 MiB of HBM per device.

```python
import jax
import jax.numpy as jnp
from jax import lax

NT = 6
BLOCK = 128
REACH = 16
NY = 1024
NX = 512


def draw_displacement(key, part):
    shape = (2, 2, NY // BLOCK, NX // BLOCK)
    offsets = jax.random.randint(key, shape, -REACH, REACH + 1, dtype=jnp.int32)
    offsets = offsets.at[:, :, 0, 0].set(REACH)
    offsets = offsets.at[:, :, NY // BLOCK - 1, NX // BLOCK - 1].set(-REACH)
    return offsets


def levels(rng, extent, split, smallest, high):
    def one(position, parts):
        steps = jax.random.uniform(jax.random.fold_in(jax.random.fold_in(rng, 6), position), (parts,), jnp.float32, smallest / len(split), high / len(split))
        return jnp.repeat(jnp.exp(steps), extent[position] // parts).reshape((-1,) + (1,) * (len(extent) - position - 1))

    gain = one(*split[0])
    for cut in split[1:]:
        gain = gain * one(*cut)
    return gain


def noise(key, shape, scale, bound, cuts=(), kind=jnp.bfloat16):
    array = jax.random.normal(key, shape, jnp.float32) * scale
    if len(cuts) > 0:
        array = levels(key, shape, cuts, -0.22, 0.18) * array
    return jnp.clip(array, min=-bound, max=bound).astype(kind)


def setup_inputs(seed: int = 0) -> dict:
    seeds = jax.random.split(jax.random.key(seed), 5)
    return {
        "tracer": noise(seeds[0], (NT, NY, NX), 1.0, 6.0, ((1, 8), (2, 4)), jnp.float32),
        "courant": jnp.clip(0.05 + 0.9 * jax.random.uniform(seeds[1], (2, 2, NY, NX), jnp.float32) ** levels(seeds[1], (2, 2, NY, NX), ((2, 8), (3, 4)), -0.2, 0.2), 0.05, 0.95),
        "displacement": draw_displacement(jax.random.fold_in(seeds[4], 71), 0),
        "cotangent": noise(seeds[3], (NT, NY, NX), 1.0, 6.0, ((1, 8), (2, 4)), jnp.float32),
    }


def lagrange_weights(fraction):
    return (-fraction * (fraction - 1.0) * (fraction - 2.0) / 6.0,
            (fraction + 1.0) * (fraction - 1.0) * (fraction - 2.0) / 2.0,
            -(fraction + 1.0) * fraction * (fraction - 2.0) / 2.0,
            (fraction + 1.0) * fraction * (fraction - 1.0) / 6.0)


def lagrange_slopes(fraction):
    square = fraction * fraction
    return (-(3.0 * square - 6.0 * fraction + 2.0) / 6.0,
            (3.0 * square - 4.0 * fraction - 1.0) / 2.0,
            -(3.0 * square - 2.0 * fraction - 2.0) / 2.0,
            (3.0 * square - 1.0) / 6.0)


def to_blocks(values, side):
    leading = values.shape[:-2]
    block_rows = values.shape[-2] // side
    block_cols = values.shape[-1] // side
    reshaped = values.reshape(leading + (block_rows, side, block_cols, side))
    count = len(leading)
    ordering = (count, count + 2) + tuple(range(count)) + (count + 1, count + 3)
    return reshaped.transpose(ordering).reshape((block_rows * block_cols,) + leading + (side, side))


def from_blocks(blocked, block_rows, block_cols):
    side = blocked.shape[-1]
    leading = blocked.shape[1:-2]
    count = len(leading)
    reshaped = blocked.reshape((block_rows, block_cols) + leading + (side, side))
    ordering = tuple(range(2, 2 + count)) + (0, count + 2, 1, count + 3)
    return reshaped.transpose(ordering).reshape(leading + (block_rows * side, block_cols * side))


def block_starts(offsets, side, halo_width):
    block_rows, block_cols = offsets.shape[1], offsets.shape[2]
    row_index = lax.broadcasted_iota(jnp.int32, (block_rows, block_cols), 0)
    col_index = lax.broadcasted_iota(jnp.int32, (block_rows, block_cols), 1)
    first_rows = (halo_width - 2 + row_index * side - offsets[0]).astype(jnp.int32).reshape(-1)
    first_cols = (halo_width - 2 + col_index * side - offsets[1]).astype(jnp.int32).reshape(-1)
    return first_rows, first_cols


def windows(padded, offsets, side, halo_width):
    first_rows, first_cols = block_starts(offsets, side, halo_width)
    tracers = padded.shape[0]

    def cutout(row_at, col_at):
        return lax.dynamic_slice(padded, (jnp.int32(0), row_at, col_at), (tracers, side + 3, side + 3))

    return jax.vmap(cutout)(first_rows, first_cols)


def advect(padded, offsets, courant_pair, side, halo_width):
    block_rows, block_cols = offsets.shape[1], offsets.shape[2]
    window_set = windows(padded, offsets, side, halo_width)
    row_weights = lagrange_weights(1.0 - to_blocks(courant_pair[0], side))
    col_weights = lagrange_weights(1.0 - to_blocks(courant_pair[1], side))
    running_sum = jnp.zeros(window_set.shape[:2] + (side, side), jnp.float32)
    for tap_row in range(4):
        for tap_col in range(4):
            factor = (row_weights[tap_row] * col_weights[tap_col])[:, None]
            running_sum = running_sum + factor * window_set[:, :, tap_row:tap_row + side, tap_col:tap_col + side]
    return from_blocks(running_sum, block_rows, block_cols)


def courant_sens(padded, offsets, courant_pair, adjoint, side, halo_width):
    block_rows, block_cols = offsets.shape[1], offsets.shape[2]
    window_set = windows(padded, offsets, side, halo_width)
    row_fraction = 1.0 - to_blocks(courant_pair[0], side)
    col_fraction = 1.0 - to_blocks(courant_pair[1], side)
    row_weights = lagrange_weights(row_fraction)
    col_weights = lagrange_weights(col_fraction)
    row_slopes = lagrange_slopes(row_fraction)
    col_slopes = lagrange_slopes(col_fraction)
    along_rows = jnp.zeros(window_set.shape[:2] + (side, side), jnp.float32)
    along_cols = jnp.zeros(window_set.shape[:2] + (side, side), jnp.float32)
    for tap_row in range(4):
        for tap_col in range(4):
            tap_values = window_set[:, :, tap_row:tap_row + side, tap_col:tap_col + side]
            along_rows = along_rows + (row_slopes[tap_row] * col_weights[tap_col])[:, None] * tap_values
            along_cols = along_cols + (row_weights[tap_row] * col_slopes[tap_col])[:, None] * tap_values
    blocked_adjoint = to_blocks(adjoint, side)
    sens_rows = -jnp.sum(blocked_adjoint * along_rows, axis=1)
    sens_cols = -jnp.sum(blocked_adjoint * along_cols, axis=1)
    return jnp.stack((from_blocks(sens_rows, block_rows, block_cols), from_blocks(sens_cols, block_rows, block_cols)))


def spread(adjoint, offsets, courant_pair, side, halo_width):
    tracers, height, width = adjoint.shape
    blocked_adjoint = to_blocks(adjoint, side)
    row_weights = lagrange_weights(1.0 - to_blocks(courant_pair[0], side))
    col_weights = lagrange_weights(1.0 - to_blocks(courant_pair[1], side))
    pieces = jnp.zeros(blocked_adjoint.shape[:2] + (side + 3, side + 3), jnp.float32)
    for tap_row in range(4):
        for tap_col in range(4):
            factor = (row_weights[tap_row] * col_weights[tap_col])[:, None]
            pieces = pieces + jnp.pad(factor * blocked_adjoint, ((0, 0), (0, 0), (tap_row, 3 - tap_row), (tap_col, 3 - tap_col)))
    first_rows, first_cols = block_starts(offsets, side, halo_width)

    def deposit(block_index, accumulator):
        corner = (jnp.int32(0), first_rows[block_index], first_cols[block_index])
        current = lax.dynamic_slice(accumulator, corner, (tracers, side + 3, side + 3))
        return lax.dynamic_update_slice(accumulator, current + pieces[block_index], corner)

    empty = jnp.zeros((tracers, height + 2 * halo_width, width + 2 * halo_width), jnp.float32)
    return lax.fori_loop(0, pieces.shape[0], deposit, empty)


def fold_periodic(padded, halo_width):
    span_cols = padded.shape[2] - 2 * halo_width
    interior = padded[:, :, halo_width:halo_width + span_cols]
    left = interior[:, :, :halo_width] + padded[:, :, halo_width + span_cols:]
    right = interior[:, :, span_cols - halo_width:] + padded[:, :, :halo_width]
    interior = jnp.concatenate((left, interior[:, :, halo_width:span_cols - halo_width], right), axis=2)
    span_rows = interior.shape[1] - 2 * halo_width
    result = interior[:, halo_width:halo_width + span_rows]
    upper = result[:, :halo_width] + interior[:, halo_width + span_rows:]
    lower = result[:, span_rows - halo_width:] + interior[:, :halo_width]
    return jnp.concatenate((upper, result[:, halo_width:span_rows - halo_width], lower), axis=1)


def reference(tracer, courant, displacement, cotangent):
    halo_width = REACH + 2
    side = BLOCK

    def wrapped(values):
        return jnp.pad(values, ((0, 0), (halo_width, halo_width), (halo_width, halo_width)), mode="wrap")

    def per_tracer(carry, pair):
        start_field = pair[0][None]
        final_adjoint = pair[1][None]
        padded_start = wrapped(start_field)
        middle = advect(padded_start, displacement[0], courant[0], side, halo_width)
        sens_late = courant_sens(wrapped(middle), displacement[1], courant[1], final_adjoint, side, halo_width)
        middle_adjoint = fold_periodic(spread(final_adjoint, displacement[1], courant[1], side, halo_width), halo_width)
        sens_early = courant_sens(padded_start, displacement[0], courant[0], middle_adjoint, side, halo_width)
        start_adjoint = fold_periodic(spread(middle_adjoint, displacement[0], courant[0], side, halo_width), halo_width)
        return carry + jnp.stack((sens_early, sens_late)), start_adjoint[0]

    initial = jnp.zeros((2, 2, NY, NX), jnp.float32)
    sensitivity, gradients = lax.scan(per_tracer, initial, (tracer, cotangent))
    return gradients, sensitivity
```

```python
import jax
import jax.numpy as jnp
from jax import lax
from jax.experimental import pallas as pl
from jax.experimental.pallas import tpu as pltpu
from jax.sharding import PartitionSpec as P

NT = 6
SIDE = 128
HALO = 24
TALL = SIDE + 2 * HALO
WIN = SIDE + 8
PITCH = 21
WIDE = 18
PAD = 40
DEEP = 216
MESH = pl.DeviceIdType.MESH


def lagrange_weights(t):
    return (
        t * (t - 1.0) * (t - 2.0) * (-1.0 / 6.0),
        (t + 1.0) * (t - 1.0) * (t - 2.0) * 0.5,
        (t + 1.0) * t * (t - 2.0) * -0.5,
        (t + 1.0) * t * (t - 1.0) * (1.0 / 6.0),
    )


def lagrange_slopes(t):
    s = t * t
    return (
        (3.0 * s - 6.0 * t + 2.0) * (-1.0 / 6.0),
        (3.0 * s - 4.0 * t - 1.0) * 0.5,
        (3.0 * s - 2.0 * t - 2.0) * -0.5,
        (3.0 * s - 1.0) * (1.0 / 6.0),
    )


def kernel(
    sizes, tracer, courant, disp, cotangent, grad, sens,
    q0, q1, s, c0, c1, w, lap, vp, eb, hb, f, fp, ma, rr, rc, rx, send, recv,
):
    nx, ny = sizes
    q, c = (q0, q1), (c0, c1)
    ix, iy = lax.axis_index("gx"), lax.axis_index("gy")
    left, right = lax.rem(ix + nx - 1, nx), lax.rem(ix + 1, nx)
    up, down = lax.rem(iy + ny - 1, ny), lax.rem(iy + 1, ny)

    barrier = pltpu.get_barrier_semaphore()
    around = (
        (left, iy), (right, iy), (ix, up), (ix, down),
        (left, up), (left, down), (right, up), (right, down),
    )
    for who in around:
        pl.semaphore_signal(barrier, inc=1, device_id=who, device_id_type=MESH)

    lane = lax.broadcasted_iota(jnp.int32, (8, SIDE), 1)
    top, main, low = pl.ds(0, HALO), pl.ds(HALO, SIDE), pl.ds(HALO + SIDE, HALO)
    first, last = pl.ds(0, HALO), pl.ds(SIDE - HALO, HALO)

    def rows(k, shift=0):
        return pl.ds(pl.multiple_of(k * 8, 8) + shift, 8)

    def make(stage, plan):
        return [
            pltpu.make_async_remote_copy(
                src_ref=src, dst_ref=dst,
                send_sem=send.at[stage, n], recv_sem=recv.at[stage, n],
                device_id=who, device_id_type=MESH,
            )
            for n, (src, dst, who) in enumerate(plan)
        ]

    def halo_copies(h):
        return make(h, (
            (s.at[h, 0], c[h].at[0, main], (left, iy)),
            (s.at[h, 1], c[h].at[1, main], (right, iy)),
            (s.at[h, 0, first], c[h].at[0, low], (left, up)),
            (s.at[h, 0, last], c[h].at[0, top], (left, down)),
            (s.at[h, 1, first], c[h].at[1, low], (right, up)),
            (s.at[h, 1, last], c[h].at[1, top], (right, down)),
            (q[h].at[:, pl.ds(HALO, HALO)], q[h].at[:, low], (ix, up)),
            (q[h].at[:, pl.ds(SIDE, HALO)], q[h].at[:, top], (ix, down)),
        ))

    def fold_copies(x):
        return make(2 + x, (
            (fp.at[x, 0, main], rc.at[x, 0], (right, iy)),
            (fp.at[x, 1, main], rc.at[x, 1], (left, iy)),
            (fp.at[x, 0, top], rx.at[x, 0, 0], (right, up)),
            (fp.at[x, 0, low], rx.at[x, 0, 1], (right, down)),
            (fp.at[x, 1, top], rx.at[x, 1, 0], (left, up)),
            (fp.at[x, 1, low], rx.at[x, 1, 1], (left, down)),
            (f.at[x, :, top], rr.at[x, 0], (ix, up)),
            (f.at[x, :, low], rr.at[x, 1], (ix, down)),
        ))

    right_lanes = [(lane >= PITCH * t) & (lane < PITCH * t + WIDE) for t in range(NT)]
    left_lanes = [
        (lane >= (PITCH * t - WIDE) % SIDE) & (lane < (PITCH * t - WIDE) % SIDE + WIDE)
        for t in range(NT)
    ]

    def turned(value, amount):
        return value if amount % SIDE == 0 else pltpu.roll(value, amount % SIDE, 1)

    def pack(values):
        near_low = jnp.zeros((8, SIDE), jnp.float32)
        near_high = near_low
        for t in range(NT):
            moved = turned(values[t], PITCH * t)
            near_low = jnp.where(right_lanes[t], moved, near_low)
            near_high = jnp.where(left_lanes[t], moved, near_high)
        return near_low, near_high

    def geometry(step):
        dy, dx = disp[step, 0, 0, 0], disp[step, 1, 0, 0]
        base = -2 - dx
        shifts = [base + b for b in range(4)]
        masks = [(lane >= v) & (lane < SIDE + v) for v in shifts]
        return dy, base, shifts, masks

    def fractions(step, k):
        return 1.0 - courant[step, 0, rows(k), :], 1.0 - courant[step, 1, rows(k), :]

    def make_windows(step):
        dy, base, shifts, masks = geometry(step)
        start = HALO - 2 - dy
        border = (lax.rem(lane, PITCH) < 3) & (lane < PITCH * NT)
        lim = jnp.where(border, -3, 0)
        take_low = lim <= base
        turns = [lax.rem(SIDE - v, SIDE) for v in shifts]

        def block(k, _):
            at = pl.ds(start + k * 8, 8)
            merged = jnp.where(take_low, c[step][0, at, :], c[step][1, at, :])
            for t in range(NT):
                side = turned(merged, -PITCH * t)
                mid = q[step][t, at, :]
                for b in range(4):
                    w[b, t, rows(k), :] = pltpu.roll(jnp.where(masks[b], mid, side), turns[b], 1)
            return 0

        lax.fori_loop(0, WIN // 8, block, 0)

    def advect():
        def block(k, _):
            ty, tx = fractions(0, k)
            la, lb = lagrange_weights(ty), lagrange_weights(tx)
            done = []
            for t in range(NT):
                total = None
                for a in range(4):
                    line = lb[0] * w[0, t, rows(k, a), :]
                    for b in range(1, 4):
                        line = line + lb[b] * w[b, t, rows(k, a), :]
                    total = la[a] * line if total is None else total + la[a] * line
                q1[t, rows(k, HALO), :] = total
                done.append(total)
            s[1, 0, rows(k), :], s[1, 1, rows(k), :] = pack(done)
            return 0

        lax.fori_loop(0, SIDE // 8, block, 0)

    def sensitivity(step, g):
        def block(k, _):
            ty, tx = fractions(step, k)
            la, lb = lagrange_weights(ty), lagrange_weights(tx)
            da, db = lagrange_slopes(ty), lagrange_slopes(tx)
            gs = [g[t, rows(k), :] for t in range(NT)]
            along_rows = along_cols = None
            for a in range(4):
                line = slope = None
                for b in range(4):
                    tap = gs[0] * w[b, 0, rows(k, a), :]
                    for t in range(1, NT):
                        tap = tap + gs[t] * w[b, t, rows(k, a), :]
                    line = lb[b] * tap if line is None else line + lb[b] * tap
                    slope = db[b] * tap if slope is None else slope + db[b] * tap
                along_rows = da[a] * line if along_rows is None else along_rows + da[a] * line
                along_cols = la[a] * slope if along_cols is None else along_cols + la[a] * slope
            sens[step, 0, rows(k), :] = -along_rows
            sens[step, 1, rows(k), :] = -along_cols
            return 0

        lax.fori_loop(0, SIDE // 8, block, 0)

    def spread(step, g, x):
        dy, base, shifts, masks = geometry(step)
        turns = [lax.rem(SIDE + v, SIDE) for v in shifts]

        def weigh(k, _):
            ty, tx = fractions(step, k)
            la, lb = lagrange_weights(ty), lagrange_weights(tx)
            for a in range(4):
                lap[a, rows(k, 8), :] = la[a]
            for t in range(NT):
                value = g[t, rows(k), :]
                for b in range(4):
                    vp[b, t, rows(k, 8), :] = lb[b] * value
            return 0

        lax.fori_loop(0, SIDE // 8, weigh, 0)

        def deposit(k, _):
            la = [lap[a, rows(k, 8 - a), :] for a in range(4)]
            rims = []
            for t in range(NT):
                mid = rim = jnp.zeros((8, SIDE), jnp.float32)
                for b in range(4):
                    total = la[0] * vp[b, t, rows(k, 8), :]
                    for a in range(1, 4):
                        total = total + la[a] * vp[b, t, rows(k, 8 - a), :]
                    moved = pltpu.roll(total, turns[b], 1)
                    mid = mid + jnp.where(masks[b], moved, 0.0)
                    rim = rim + jnp.where(masks[b], 0.0, moved)
                eb[t, rows(k, PAD), :] = mid
                rims.append(rim)
            hb[0, rows(k, PAD), :], hb[1, rows(k, PAD), :] = pack(rims)
            return 0

        lax.fori_loop(0, WIN // 8, deposit, 0)
        start = PAD - HALO + 2 + dy

        def place(k, _):
            at = pl.ds(start + k * 8, 8)
            for t in range(NT):
                f[x, t, rows(k), :] = eb[t, at, :]
            for d in range(2):
                fp[x, d, rows(k), :] = hb[d, at, :]
            return 0

        lax.fori_loop(0, TALL // 8, place, 0)

    def fold(x, out):
        for d in range(2):
            rc[x, d, last, :] += rx[x, d, 0]
            rc[x, d, first, :] += rx[x, d, 1]
        for t in range(NT):
            f[x, t, pl.ds(SIDE, HALO), :] += rr[x, 0, t]
            f[x, t, pl.ds(HALO, HALO), :] += rr[x, 1, t]

        def block(k, _):
            from_left, from_right = rc[x, 0, rows(k), :], rc[x, 1, rows(k), :]
            for t in range(NT):
                low_part = turned(jnp.where(right_lanes[t], from_left, 0.0), -PITCH * t)
                high_part = turned(jnp.where(left_lanes[t], from_right, 0.0), -PITCH * t)
                out[t, rows(k), :] = f[x, t, rows(k, HALO), :] + low_part + high_part
            return 0

        lax.fori_loop(0, SIDE // 8, block, 0)

    def first_pack(k, _):
        values = [tracer[t, rows(k), :] for t in range(NT)]
        for t in range(NT):
            q0[t, rows(k, HALO), :] = values[t]
        s[0, 0, rows(k), :], s[0, 1, rows(k), :] = pack(values)
        return 0

    lax.fori_loop(0, SIDE // 8, first_pack, 0)
    pl.semaphore_wait(barrier, 8)
    halo0 = halo_copies(0)
    for copy in halo0:
        copy.start()

    lap[:, 0:8, :] = jnp.zeros((4, 8, SIDE), jnp.float32)
    lap[:, SIDE + 8:, :] = jnp.zeros((4, 8, SIDE), jnp.float32)
    vp[:, :, 0:8, :] = jnp.zeros((4, NT, 8, SIDE), jnp.float32)
    vp[:, :, SIDE + 8:, :] = jnp.zeros((4, NT, 8, SIDE), jnp.float32)
    eb[:, 0:PAD, :] = jnp.zeros((NT, PAD, SIDE), jnp.float32)
    eb[:, PAD + WIN:, :] = jnp.zeros((NT, DEEP - PAD - WIN, SIDE), jnp.float32)
    hb[:, 0:PAD, :] = jnp.zeros((2, PAD, SIDE), jnp.float32)
    hb[:, PAD + WIN:, :] = jnp.zeros((2, DEEP - PAD - WIN, SIDE), jnp.float32)

    spread(1, cotangent, 0)
    fold0 = fold_copies(0)
    for copy in fold0:
        copy.start()

    for copy in halo0:
        copy.wait_recv()
    make_windows(0)
    advect()
    halo1 = halo_copies(1)
    for copy in halo1:
        copy.start()

    for copy in fold0:
        copy.wait()
    fold(0, ma)
    spread(0, ma, 1)
    fold1 = fold_copies(1)
    for copy in fold1:
        copy.start()
    sensitivity(0, ma)

    for copy in halo1:
        copy.wait_recv()
    make_windows(1)
    sensitivity(1, cotangent)

    for copy in fold1:
        copy.wait()
    fold(1, grad)
    for copy in halo0 + halo1:
        copy.wait_send()


def solution(mesh):
    sizes = (mesh.shape["gx"], mesh.shape["gy"])
    f32 = jnp.float32

    def body(tracer, courant, displacement, cotangent):
        vmem = pl.BlockSpec(memory_space=pltpu.VMEM)
        return pl.pallas_call(
            lambda *refs: kernel(sizes, *refs),
            out_shape=(
                jax.ShapeDtypeStruct((NT, SIDE, SIDE), f32),
                jax.ShapeDtypeStruct((2, 2, SIDE, SIDE), f32),
            ),
            in_specs=[vmem, vmem, pl.BlockSpec(memory_space=pltpu.SMEM), vmem],
            out_specs=(vmem, vmem),
            scratch_shapes=[
                pltpu.VMEM((NT, TALL, SIDE), f32),
                pltpu.VMEM((NT, TALL, SIDE), f32),
                pltpu.VMEM((2, 2, SIDE, SIDE), f32),
                pltpu.VMEM((2, TALL, SIDE), f32),
                pltpu.VMEM((2, TALL, SIDE), f32),
                pltpu.VMEM((4, NT, WIN, SIDE), f32),
                pltpu.VMEM((4, SIDE + 16, SIDE), f32),
                pltpu.VMEM((4, NT, SIDE + 16, SIDE), f32),
                pltpu.VMEM((NT, DEEP, SIDE), f32),
                pltpu.VMEM((2, DEEP, SIDE), f32),
                pltpu.VMEM((2, NT, TALL, SIDE), f32),
                pltpu.VMEM((2, 2, TALL, SIDE), f32),
                pltpu.VMEM((NT, SIDE, SIDE), f32),
                pltpu.VMEM((2, 2, NT, HALO, SIDE), f32),
                pltpu.VMEM((2, 2, SIDE, SIDE), f32),
                pltpu.VMEM((2, 2, 2, HALO, SIDE), f32),
                pltpu.SemaphoreType.DMA((4, 8)),
                pltpu.SemaphoreType.DMA((4, 8)),
            ],
            compiler_params=pltpu.CompilerParams(
                collective_id=0, has_side_effects=True, vmem_limit_bytes=48 * 1024 * 1024
            ),
        )(tracer, courant, displacement, cotangent)

    in_specs = (
        P(None, "gy", "gx"),
        P(None, None, "gy", "gx"),
        P(None, None, "gy", "gx"),
        P(None, "gy", "gx"),
    )
    out_specs = (P(None, "gy", "gx"), P(None, None, "gy", "gx"))
    return jax.shard_map(body, mesh=mesh, in_specs=in_specs, out_specs=out_specs, check_vma=False)
```

```python
import jax
import jax.numpy as jnp
from jax import lax
from jax.experimental import pallas as pl
from jax.experimental.pallas import tpu as pltpu
from jax.sharding import PartitionSpec as P

NT = 6
SIDE = 128
HALO = 24
TALL = SIDE + 2 * HALO
WIN = SIDE + 8
PITCH = 21
WIDE = 18
PAD = 40
DEEP = 216
MESH = pl.DeviceIdType.MESH


def lagrange_weights(t):
    return (
        t * (t - 1.0) * (t - 2.0) * (-1.0 / 6.0),
        (t + 1.0) * (t - 1.0) * (t - 2.0) * 0.5,
        (t + 1.0) * t * (t - 2.0) * -0.5,
        (t + 1.0) * t * (t - 1.0) * (1.0 / 6.0),
    )


def lagrange_slopes(t):
    s = t * t
    return (
        (3.0 * s - 6.0 * t + 2.0) * (-1.0 / 6.0),
        (3.0 * s - 4.0 * t - 1.0) * 0.5,
        (3.0 * s - 2.0 * t - 2.0) * -0.5,
        (3.0 * s - 1.0) * (1.0 / 6.0),
    )


def kernel(
    sizes, tracer_in, courant_in, disp_in, cotangent_in, grad, sens,
    courant, disp, cotangent, q0, q1, s, c0, c1, w, lap, vp, eb, hb, f, fp, ma, rr, rc, rx, send, recv, load,
):
    nx, ny = sizes
    q, c = (q0, q1), (c0, c1)
    ix, iy = lax.axis_index("gx"), lax.axis_index("gy")
    left, right = lax.rem(ix + nx - 1, nx), lax.rem(ix + 1, nx)
    up, down = lax.rem(iy + ny - 1, ny), lax.rem(iy + 1, ny)

    loads = [
        pltpu.make_async_copy(src, dst, load.at[n])
        for n, (src, dst) in enumerate((
            (tracer_in, q0.at[:, pl.ds(HALO, SIDE)]),
            (disp_in, disp),
            (courant_in, courant),
            (cotangent_in, cotangent),
        ))
    ]
    for copy in loads:
        copy.start()

    barrier = pltpu.get_barrier_semaphore()
    around = (
        (left, iy), (right, iy), (ix, up), (ix, down),
        (left, up), (left, down), (right, up), (right, down),
    )
    for who in around:
        pl.semaphore_signal(barrier, inc=1, device_id=who, device_id_type=MESH)

    lane = lax.broadcasted_iota(jnp.int32, (8, SIDE), 1)
    top, main, low = pl.ds(0, HALO), pl.ds(HALO, SIDE), pl.ds(HALO + SIDE, HALO)
    first, last = pl.ds(0, HALO), pl.ds(SIDE - HALO, HALO)

    def rows(k, shift=0):
        return pl.ds(pl.multiple_of(k * 8, 8) + shift, 8)

    def make(stage, plan):
        return [
            pltpu.make_async_remote_copy(
                src_ref=src, dst_ref=dst,
                send_sem=send.at[stage, n], recv_sem=recv.at[stage, n],
                device_id=who, device_id_type=MESH,
            )
            for n, (src, dst, who) in enumerate(plan)
        ]

    def halo_copies(h):
        return make(h, (
            (s.at[h, 0], c[h].at[0, main], (left, iy)),
            (s.at[h, 1], c[h].at[1, main], (right, iy)),
            (s.at[h, 0, first], c[h].at[0, low], (left, up)),
            (s.at[h, 0, last], c[h].at[0, top], (left, down)),
            (s.at[h, 1, first], c[h].at[1, low], (right, up)),
            (s.at[h, 1, last], c[h].at[1, top], (right, down)),
            (q[h].at[:, pl.ds(HALO, HALO)], q[h].at[:, low], (ix, up)),
            (q[h].at[:, pl.ds(SIDE, HALO)], q[h].at[:, top], (ix, down)),
        ))

    def fold_copies(x):
        return make(2 + x, (
            (fp.at[x, 0, main], rc.at[x, 0], (right, iy)),
            (fp.at[x, 1, main], rc.at[x, 1], (left, iy)),
            (fp.at[x, 0, top], rx.at[x, 0, 0], (right, up)),
            (fp.at[x, 0, low], rx.at[x, 0, 1], (right, down)),
            (fp.at[x, 1, top], rx.at[x, 1, 0], (left, up)),
            (fp.at[x, 1, low], rx.at[x, 1, 1], (left, down)),
            (f.at[x, :, top], rr.at[x, 0], (ix, up)),
            (f.at[x, :, low], rr.at[x, 1], (ix, down)),
        ))

    right_lanes = [(lane >= PITCH * t) & (lane < PITCH * t + WIDE) for t in range(NT)]
    left_lanes = [
        (lane >= (PITCH * t - WIDE) % SIDE) & (lane < (PITCH * t - WIDE) % SIDE + WIDE)
        for t in range(NT)
    ]

    def turned(value, amount):
        return value if amount % SIDE == 0 else pltpu.roll(value, amount % SIDE, 1)

    def pack(values):
        near_low = jnp.zeros((8, SIDE), jnp.float32)
        near_high = near_low
        for t in range(NT):
            moved = turned(values[t], PITCH * t)
            near_low = jnp.where(right_lanes[t], moved, near_low)
            near_high = jnp.where(left_lanes[t], moved, near_high)
        return near_low, near_high

    def geometry(step):
        dy, dx = disp[step, 0, 0, 0], disp[step, 0, 0, 1]
        base = -2 - dx
        shifts = [base + b for b in range(4)]
        masks = [(lane >= v) & (lane < SIDE + v) for v in shifts]
        return dy, base, shifts, masks

    def fractions(step, k):
        return 1.0 - courant[step, 0, rows(k), :], 1.0 - courant[step, 1, rows(k), :]

    def make_windows(step):
        dy, base, shifts, masks = geometry(step)
        start = HALO - 2 - dy
        border = (lax.rem(lane, PITCH) < 3) & (lane < PITCH * NT)
        lim = jnp.where(border, -3, 0)
        take_low = lim <= base
        turns = [lax.rem(SIDE - v, SIDE) for v in shifts]

        def block(k, _):
            at = pl.ds(start + k * 8, 8)
            merged = jnp.where(take_low, c[step][0, at, :], c[step][1, at, :])
            for t in range(NT):
                side = turned(merged, -PITCH * t)
                mid = q[step][t, at, :]
                for b in range(4):
                    w[b, t, rows(k), :] = pltpu.roll(jnp.where(masks[b], mid, side), turns[b], 1)
            return 0

        lax.fori_loop(0, WIN // 8, block, 0)

    def advect():
        def block(k, _):
            ty, tx = fractions(0, k)
            la, lb = lagrange_weights(ty), lagrange_weights(tx)
            done = []
            for t in range(NT):
                total = None
                for a in range(4):
                    line = lb[0] * w[0, t, rows(k, a), :]
                    for b in range(1, 4):
                        line = line + lb[b] * w[b, t, rows(k, a), :]
                    total = la[a] * line if total is None else total + la[a] * line
                q1[t, rows(k, HALO), :] = total
                done.append(total)
            s[1, 0, rows(k), :], s[1, 1, rows(k), :] = pack(done)
            return 0

        lax.fori_loop(0, SIDE // 8, block, 0)

    def sensitivity(step, g):
        def block(k, _):
            ty, tx = fractions(step, k)
            la, lb = lagrange_weights(ty), lagrange_weights(tx)
            da, db = lagrange_slopes(ty), lagrange_slopes(tx)
            gs = [g[t, rows(k), :] for t in range(NT)]
            along_rows = along_cols = None
            for a in range(4):
                line = slope = None
                for b in range(4):
                    tap = gs[0] * w[b, 0, rows(k, a), :]
                    for t in range(1, NT):
                        tap = tap + gs[t] * w[b, t, rows(k, a), :]
                    line = lb[b] * tap if line is None else line + lb[b] * tap
                    slope = db[b] * tap if slope is None else slope + db[b] * tap
                along_rows = da[a] * line if along_rows is None else along_rows + da[a] * line
                along_cols = la[a] * slope if along_cols is None else along_cols + la[a] * slope
            sens[step, 0, rows(k), :] = -along_rows
            sens[step, 1, rows(k), :] = -along_cols
            return 0

        lax.fori_loop(0, SIDE // 8, block, 0)

    def spread(step, g, x):
        dy, base, shifts, masks = geometry(step)
        turns = [lax.rem(SIDE + v, SIDE) for v in shifts]

        def weigh(k, _):
            ty, tx = fractions(step, k)
            la, lb = lagrange_weights(ty), lagrange_weights(tx)
            for a in range(4):
                lap[a, rows(k, 8), :] = la[a]
            for t in range(NT):
                value = g[t, rows(k), :]
                for b in range(4):
                    vp[b, t, rows(k, 8), :] = lb[b] * value
            return 0

        lax.fori_loop(0, SIDE // 8, weigh, 0)

        def deposit(k, _):
            la = [lap[a, rows(k, 8 - a), :] for a in range(4)]
            rims = []
            for t in range(NT):
                mid = rim = jnp.zeros((8, SIDE), jnp.float32)
                for b in range(4):
                    total = la[0] * vp[b, t, rows(k, 8), :]
                    for a in range(1, 4):
                        total = total + la[a] * vp[b, t, rows(k, 8 - a), :]
                    moved = pltpu.roll(total, turns[b], 1)
                    mid = mid + jnp.where(masks[b], moved, 0.0)
                    rim = rim + jnp.where(masks[b], 0.0, moved)
                eb[t, rows(k, PAD), :] = mid
                rims.append(rim)
            hb[0, rows(k, PAD), :], hb[1, rows(k, PAD), :] = pack(rims)
            return 0

        lax.fori_loop(0, WIN // 8, deposit, 0)
        start = PAD - HALO + 2 + dy

        def place(k, _):
            at = pl.ds(start + k * 8, 8)
            for t in range(NT):
                f[x, t, rows(k), :] = eb[t, at, :]
            for d in range(2):
                fp[x, d, rows(k), :] = hb[d, at, :]
            return 0

        lax.fori_loop(0, TALL // 8, place, 0)

    def fold(x, out):
        for d in range(2):
            rc[x, d, last, :] += rx[x, d, 0]
            rc[x, d, first, :] += rx[x, d, 1]
        for t in range(NT):
            f[x, t, pl.ds(SIDE, HALO), :] += rr[x, 0, t]
            f[x, t, pl.ds(HALO, HALO), :] += rr[x, 1, t]

        def block(k, _):
            from_left, from_right = rc[x, 0, rows(k), :], rc[x, 1, rows(k), :]
            for t in range(NT):
                low_part = turned(jnp.where(right_lanes[t], from_left, 0.0), -PITCH * t)
                high_part = turned(jnp.where(left_lanes[t], from_right, 0.0), -PITCH * t)
                out[t, rows(k), :] = f[x, t, rows(k, HALO), :] + low_part + high_part
            return 0

        lax.fori_loop(0, SIDE // 8, block, 0)

    def first_pack(k, _):
        values = [q0[t, rows(k, HALO), :] for t in range(NT)]
        s[0, 0, rows(k), :], s[0, 1, rows(k), :] = pack(values)
        return 0

    loads[0].wait()
    lax.fori_loop(0, SIDE // 8, first_pack, 0)
    pl.semaphore_wait(barrier, 8)
    halo0 = halo_copies(0)
    for copy in halo0:
        copy.start()

    lap[:, 0:8, :] = jnp.zeros((4, 8, SIDE), jnp.float32)
    lap[:, SIDE + 8:, :] = jnp.zeros((4, 8, SIDE), jnp.float32)
    vp[:, :, 0:8, :] = jnp.zeros((4, NT, 8, SIDE), jnp.float32)
    vp[:, :, SIDE + 8:, :] = jnp.zeros((4, NT, 8, SIDE), jnp.float32)
    eb[:, 0:PAD, :] = jnp.zeros((NT, PAD, SIDE), jnp.float32)
    eb[:, PAD + WIN:, :] = jnp.zeros((NT, DEEP - PAD - WIN, SIDE), jnp.float32)
    hb[:, 0:PAD, :] = jnp.zeros((2, PAD, SIDE), jnp.float32)
    hb[:, PAD + WIN:, :] = jnp.zeros((2, DEEP - PAD - WIN, SIDE), jnp.float32)

    for copy in loads[1:]:
        copy.wait()
    spread(1, cotangent, 0)
    fold0 = fold_copies(0)
    for copy in fold0:
        copy.start()

    for copy in halo0:
        copy.wait_recv()
    make_windows(0)
    advect()
    halo1 = halo_copies(1)
    for copy in halo1:
        copy.start()

    for copy in fold0:
        copy.wait()
    fold(0, ma)
    spread(0, ma, 1)
    fold1 = fold_copies(1)
    for copy in fold1:
        copy.start()
    sensitivity(0, ma)

    for copy in halo1:
        copy.wait_recv()
    make_windows(1)
    sensitivity(1, cotangent)

    for copy in fold1:
        copy.wait()
    fold(1, grad)
    for copy in halo0 + halo1:
        copy.wait_send()


def solution(mesh):
    sizes = (mesh.shape["gx"], mesh.shape["gy"])
    f32 = jnp.float32

    def body(tracer, courant, displacement, cotangent):
        vmem = pl.BlockSpec(memory_space=pltpu.VMEM)
        return pl.pallas_call(
            lambda *refs: kernel(sizes, *refs),
            out_shape=(
                jax.ShapeDtypeStruct((NT, SIDE, SIDE), f32),
                jax.ShapeDtypeStruct((2, 2, SIDE, SIDE), f32),
            ),
            in_specs=[pl.BlockSpec(memory_space=pl.ANY)] * 4,
            out_specs=(vmem, vmem),
            scratch_shapes=[
                pltpu.VMEM((2, 2, SIDE, SIDE), f32),
                pltpu.SMEM((2, 1, 1, 2), jnp.int32),
                pltpu.VMEM((NT, SIDE, SIDE), f32),
                pltpu.VMEM((NT, TALL, SIDE), f32),
                pltpu.VMEM((NT, TALL, SIDE), f32),
                pltpu.VMEM((2, 2, SIDE, SIDE), f32),
                pltpu.VMEM((2, TALL, SIDE), f32),
                pltpu.VMEM((2, TALL, SIDE), f32),
                pltpu.VMEM((4, NT, WIN, SIDE), f32),
                pltpu.VMEM((4, SIDE + 16, SIDE), f32),
                pltpu.VMEM((4, NT, SIDE + 16, SIDE), f32),
                pltpu.VMEM((NT, DEEP, SIDE), f32),
                pltpu.VMEM((2, DEEP, SIDE), f32),
                pltpu.VMEM((2, NT, TALL, SIDE), f32),
                pltpu.VMEM((2, 2, TALL, SIDE), f32),
                pltpu.VMEM((NT, SIDE, SIDE), f32),
                pltpu.VMEM((2, 2, NT, HALO, SIDE), f32),
                pltpu.VMEM((2, 2, SIDE, SIDE), f32),
                pltpu.VMEM((2, 2, 2, HALO, SIDE), f32),
                pltpu.SemaphoreType.DMA((4, 8)),
                pltpu.SemaphoreType.DMA((4, 8)),
                pltpu.SemaphoreType.DMA((4,)),
            ],
            compiler_params=pltpu.CompilerParams(
                collective_id=0, has_side_effects=True, vmem_limit_bytes=62 * 1024 * 1024
            ),
        )(tracer, courant, displacement.transpose(0, 2, 3, 1), cotangent)

    in_specs = (
        P(None, "gy", "gx"),
        P(None, None, "gy", "gx"),
        P(None, None, "gy", "gx"),
        P(None, "gy", "gx"),
    )
    out_specs = (P(None, "gy", "gx"), P(None, None, "gy", "gx"))
    return jax.shard_map(body, mesh=mesh, in_specs=in_specs, out_specs=out_specs, check_vma=False)
```

```python
import jax
import jax.numpy as jnp
from jax import lax
from jax.experimental import pallas as pl
from jax.experimental.pallas import tpu as pltpu
from jax.sharding import PartitionSpec as P

NT = 6
SIDE = 128
HALO = 24
TALL = SIDE + 2 * HALO
WIN = SIDE + 8
PITCH = 21
WIDE = 18
PAD = 40
DEEP = 216
MESH = pl.DeviceIdType.MESH


def lagrange_weights(t):
    return (
        t * (t - 1.0) * (t - 2.0) * (-1.0 / 6.0),
        (t + 1.0) * (t - 1.0) * (t - 2.0) * 0.5,
        (t + 1.0) * t * (t - 2.0) * -0.5,
        (t + 1.0) * t * (t - 1.0) * (1.0 / 6.0),
    )


def lagrange_slopes(t):
    s = t * t
    return (
        (3.0 * s - 6.0 * t + 2.0) * (-1.0 / 6.0),
        (3.0 * s - 4.0 * t - 1.0) * 0.5,
        (3.0 * s - 2.0 * t - 2.0) * -0.5,
        (3.0 * s - 1.0) * (1.0 / 6.0),
    )


def kernel(
    sizes, tracer_in, courant_in, disp_in, cotangent_in, grad, sens,
    courant, disp, cotangent, q0, q1, s, c0, c1, w, lap, vp, eb, hb, f, fp, ma, rr, rc, rx, send, recv, load,
):
    nx, ny = sizes
    q, c = (q0, q1), (c0, c1)
    ix, iy = lax.axis_index("gx"), lax.axis_index("gy")
    left, right = lax.rem(ix + nx - 1, nx), lax.rem(ix + 1, nx)
    up, down = lax.rem(iy + ny - 1, ny), lax.rem(iy + 1, ny)

    loads = [
        pltpu.make_async_copy(src, dst, load.at[n])
        for n, (src, dst) in enumerate((
            (tracer_in, q0.at[:, pl.ds(HALO, SIDE)]),
            (disp_in, disp),
            (courant_in, courant),
            (cotangent_in, cotangent),
        ))
    ]
    for copy in loads:
        copy.start()

    barrier = pltpu.get_barrier_semaphore()
    around = ((left, iy), (right, iy), (ix, up), (ix, down))
    for who in around:
        pl.semaphore_signal(barrier, inc=1, device_id=who, device_id_type=MESH)

    lane = lax.broadcasted_iota(jnp.int32, (8, SIDE), 1)
    top, main, low = pl.ds(0, HALO), pl.ds(HALO, SIDE), pl.ds(HALO + SIDE, HALO)


    def rows(k, shift=0):
        return pl.ds(pl.multiple_of(k * 8, 8) + shift, 8)

    def make(stage, base, plan):
        return [
            pltpu.make_async_remote_copy(
                src_ref=src, dst_ref=dst,
                send_sem=send.at[stage, base + n], recv_sem=recv.at[stage, base + n],
                device_id=who, device_id_type=MESH,
            )
            for n, (src, dst, who) in enumerate(plan)
        ]

    def halo_copies(h):
        return make(h, 0, (
            (s.at[h, 0], c[h].at[0, main], (left, iy)),
            (s.at[h, 1], c[h].at[1, main], (right, iy)),
            (q[h].at[:, pl.ds(HALO, HALO)], q[h].at[:, low], (ix, up)),
            (q[h].at[:, pl.ds(SIDE, HALO)], q[h].at[:, top], (ix, down)),
        ))

    def corner_copies(h):
        return make(h, 4, (
            (c[h].at[:, pl.ds(HALO, HALO)], c[h].at[:, low], (ix, up)),
            (c[h].at[:, pl.ds(SIDE, HALO)], c[h].at[:, top], (ix, down)),
        ))

    def fold_rows(x):
        return make(2 + x, 0, (
            (fp.at[x, :, top], rx.at[x, 0], (ix, up)),
            (fp.at[x, :, low], rx.at[x, 1], (ix, down)),
            (f.at[x, :, top], rr.at[x, 0], (ix, up)),
            (f.at[x, :, low], rr.at[x, 1], (ix, down)),
        ))

    def fold_columns(x):
        return make(2 + x, 4, (
            (fp.at[x, 0, main], rc.at[x, 0], (right, iy)),
            (fp.at[x, 1, main], rc.at[x, 1], (left, iy)),
        ))

    right_lanes = [(lane >= PITCH * t) & (lane < PITCH * t + WIDE) for t in range(NT)]
    left_lanes = [
        (lane >= (PITCH * t - WIDE) % SIDE) & (lane < (PITCH * t - WIDE) % SIDE + WIDE)
        for t in range(NT)
    ]

    def go(copies):
        for copy in copies:
            copy.start()

    def arrive(copies):
        for copy in copies:
            copy.wait_recv()

    def forward(h, copies):
        arrive(copies[:2])
        corners = corner_copies(h)
        go(corners)
        return corners

    def relay(x, copies):
        arrive(copies[:2])
        for d in range(2):
            fp[x, d, pl.ds(SIDE, HALO), :] += rx[x, 0, d]
            fp[x, d, pl.ds(HALO, HALO), :] += rx[x, 1, d]
        columns = fold_columns(x)
        go(columns)
        return columns

    def turned(value, amount):
        return value if amount % SIDE == 0 else pltpu.roll(value, amount % SIDE, 1)

    def pack(values):
        near_low = jnp.zeros((8, SIDE), jnp.float32)
        near_high = near_low
        for t in range(NT):
            moved = turned(values[t], PITCH * t)
            near_low = jnp.where(right_lanes[t], moved, near_low)
            near_high = jnp.where(left_lanes[t], moved, near_high)
        return near_low, near_high

    def geometry(step):
        dy, dx = disp[step, 0, 0, 0], disp[step, 0, 0, 1]
        base = -2 - dx
        shifts = [base + b for b in range(4)]
        masks = [(lane >= v) & (lane < SIDE + v) for v in shifts]
        return dy, base, shifts, masks

    def fractions(step, k):
        return 1.0 - courant[step, 0, rows(k), :], 1.0 - courant[step, 1, rows(k), :]

    def make_windows(step):
        dy, base, shifts, masks = geometry(step)
        start = HALO - 2 - dy
        border = (lax.rem(lane, PITCH) < 3) & (lane < PITCH * NT)
        lim = jnp.where(border, -3, 0)
        take_low = lim <= base
        turns = [lax.rem(SIDE - v, SIDE) for v in shifts]

        def block(k, _):
            at = pl.ds(start + k * 8, 8)
            merged = jnp.where(take_low, c[step][0, at, :], c[step][1, at, :])
            for t in range(NT):
                side = turned(merged, -PITCH * t)
                mid = q[step][t, at, :]
                for b in range(4):
                    w[b, t, rows(k), :] = pltpu.roll(jnp.where(masks[b], mid, side), turns[b], 1)
            return 0

        lax.fori_loop(0, WIN // 8, block, 0)

    def advect():
        def block(k, _):
            ty, tx = fractions(0, k)
            la, lb = lagrange_weights(ty), lagrange_weights(tx)
            done = []
            for t in range(NT):
                total = None
                for a in range(4):
                    line = lb[0] * w[0, t, rows(k, a), :]
                    for b in range(1, 4):
                        line = line + lb[b] * w[b, t, rows(k, a), :]
                    total = la[a] * line if total is None else total + la[a] * line
                q1[t, rows(k, HALO), :] = total
                done.append(total)
            s[1, 0, rows(k), :], s[1, 1, rows(k), :] = pack(done)
            return 0

        lax.fori_loop(0, SIDE // 8, block, 0)

    def sensitivity(step, g):
        def block(k, _):
            ty, tx = fractions(step, k)
            la, lb = lagrange_weights(ty), lagrange_weights(tx)
            da, db = lagrange_slopes(ty), lagrange_slopes(tx)
            gs = [g[t, rows(k), :] for t in range(NT)]
            along_rows = along_cols = None
            for a in range(4):
                line = slope = None
                for b in range(4):
                    tap = gs[0] * w[b, 0, rows(k, a), :]
                    for t in range(1, NT):
                        tap = tap + gs[t] * w[b, t, rows(k, a), :]
                    line = lb[b] * tap if line is None else line + lb[b] * tap
                    slope = db[b] * tap if slope is None else slope + db[b] * tap
                along_rows = da[a] * line if along_rows is None else along_rows + da[a] * line
                along_cols = la[a] * slope if along_cols is None else along_cols + la[a] * slope
            sens[step, 0, rows(k), :] = -along_rows
            sens[step, 1, rows(k), :] = -along_cols
            return 0

        lax.fori_loop(0, SIDE // 8, block, 0)

    def spread(step, g, x):
        dy, base, shifts, masks = geometry(step)
        turns = [lax.rem(SIDE + v, SIDE) for v in shifts]

        def weigh(k, _):
            ty, tx = fractions(step, k)
            la, lb = lagrange_weights(ty), lagrange_weights(tx)
            for a in range(4):
                lap[a, rows(k, 8), :] = la[a]
            for t in range(NT):
                value = g[t, rows(k), :]
                for b in range(4):
                    vp[b, t, rows(k, 8), :] = lb[b] * value
            return 0

        lax.fori_loop(0, SIDE // 8, weigh, 0)

        def deposit(k, _):
            la = [lap[a, rows(k, 8 - a), :] for a in range(4)]
            rims = []
            for t in range(NT):
                mid = rim = jnp.zeros((8, SIDE), jnp.float32)
                for b in range(4):
                    total = la[0] * vp[b, t, rows(k, 8), :]
                    for a in range(1, 4):
                        total = total + la[a] * vp[b, t, rows(k, 8 - a), :]
                    moved = pltpu.roll(total, turns[b], 1)
                    mid = mid + jnp.where(masks[b], moved, 0.0)
                    rim = rim + jnp.where(masks[b], 0.0, moved)
                eb[t, rows(k, PAD), :] = mid
                rims.append(rim)
            hb[0, rows(k, PAD), :], hb[1, rows(k, PAD), :] = pack(rims)
            return 0

        lax.fori_loop(0, WIN // 8, deposit, 0)
        start = PAD - HALO + 2 + dy

        def place(k, _):
            at = pl.ds(start + k * 8, 8)
            for t in range(NT):
                f[x, t, rows(k), :] = eb[t, at, :]
            for d in range(2):
                fp[x, d, rows(k), :] = hb[d, at, :]
            return 0

        lax.fori_loop(0, TALL // 8, place, 0)

    def fold(x, out):
        for t in range(NT):
            f[x, t, pl.ds(SIDE, HALO), :] += rr[x, 0, t]
            f[x, t, pl.ds(HALO, HALO), :] += rr[x, 1, t]

        def block(k, _):
            from_left, from_right = rc[x, 0, rows(k), :], rc[x, 1, rows(k), :]
            for t in range(NT):
                low_part = turned(jnp.where(right_lanes[t], from_left, 0.0), -PITCH * t)
                high_part = turned(jnp.where(left_lanes[t], from_right, 0.0), -PITCH * t)
                out[t, rows(k), :] = f[x, t, rows(k, HALO), :] + low_part + high_part
            return 0

        lax.fori_loop(0, SIDE // 8, block, 0)

    def first_pack(k, _):
        values = [q0[t, rows(k, HALO), :] for t in range(NT)]
        s[0, 0, rows(k), :], s[0, 1, rows(k), :] = pack(values)
        return 0

    loads[0].wait()
    lax.fori_loop(0, SIDE // 8, first_pack, 0)
    pl.semaphore_wait(barrier, 4)
    halo0 = halo_copies(0)
    go(halo0)

    lap[:, 0:8, :] = jnp.zeros((4, 8, SIDE), jnp.float32)
    lap[:, SIDE + 8:, :] = jnp.zeros((4, 8, SIDE), jnp.float32)
    vp[:, :, 0:8, :] = jnp.zeros((4, NT, 8, SIDE), jnp.float32)
    vp[:, :, SIDE + 8:, :] = jnp.zeros((4, NT, 8, SIDE), jnp.float32)
    eb[:, 0:PAD, :] = jnp.zeros((NT, PAD, SIDE), jnp.float32)
    eb[:, PAD + WIN:, :] = jnp.zeros((NT, DEEP - PAD - WIN, SIDE), jnp.float32)
    hb[:, 0:PAD, :] = jnp.zeros((2, PAD, SIDE), jnp.float32)
    hb[:, PAD + WIN:, :] = jnp.zeros((2, DEEP - PAD - WIN, SIDE), jnp.float32)

    for copy in loads[1:]:
        copy.wait()
    spread(1, cotangent, 0)
    rows0 = fold_rows(0)
    go(rows0)
    corners0 = forward(0, halo0)
    columns0 = relay(0, rows0)

    arrive(halo0[2:] + corners0)
    make_windows(0)
    advect()
    halo1 = halo_copies(1)
    go(halo1)

    arrive(rows0[2:] + columns0)
    fold(0, ma)
    spread(0, ma, 1)
    rows1 = fold_rows(1)
    go(rows1)
    corners1 = forward(1, halo1)
    columns1 = relay(1, rows1)
    sensitivity(0, ma)

    arrive(halo1[2:] + corners1)
    make_windows(1)
    sensitivity(1, cotangent)

    arrive(rows1[2:] + columns1)
    fold(1, grad)
    for copy in halo0 + corners0 + rows0 + columns0 + halo1 + corners1 + rows1 + columns1:
        copy.wait_send()


def solution(mesh):
    sizes = (mesh.shape["gx"], mesh.shape["gy"])
    f32 = jnp.float32

    def body(tracer, courant, displacement, cotangent):
        vmem = pl.BlockSpec(memory_space=pltpu.VMEM)
        return pl.pallas_call(
            lambda *refs: kernel(sizes, *refs),
            out_shape=(
                jax.ShapeDtypeStruct((NT, SIDE, SIDE), f32),
                jax.ShapeDtypeStruct((2, 2, SIDE, SIDE), f32),
            ),
            in_specs=[pl.BlockSpec(memory_space=pl.ANY)] * 4,
            out_specs=(vmem, vmem),
            scratch_shapes=[
                pltpu.VMEM((2, 2, SIDE, SIDE), f32),
                pltpu.SMEM((2, 1, 1, 2), jnp.int32),
                pltpu.VMEM((NT, SIDE, SIDE), f32),
                pltpu.VMEM((NT, TALL, SIDE), f32),
                pltpu.VMEM((NT, TALL, SIDE), f32),
                pltpu.VMEM((2, 2, SIDE, SIDE), f32),
                pltpu.VMEM((2, TALL, SIDE), f32),
                pltpu.VMEM((2, TALL, SIDE), f32),
                pltpu.VMEM((4, NT, WIN, SIDE), f32),
                pltpu.VMEM((4, SIDE + 16, SIDE), f32),
                pltpu.VMEM((4, NT, SIDE + 16, SIDE), f32),
                pltpu.VMEM((NT, DEEP, SIDE), f32),
                pltpu.VMEM((2, DEEP, SIDE), f32),
                pltpu.VMEM((2, NT, TALL, SIDE), f32),
                pltpu.VMEM((2, 2, TALL, SIDE), f32),
                pltpu.VMEM((NT, SIDE, SIDE), f32),
                pltpu.VMEM((2, 2, NT, HALO, SIDE), f32),
                pltpu.VMEM((2, 2, SIDE, SIDE), f32),
                pltpu.VMEM((2, 2, 2, HALO, SIDE), f32),
                pltpu.SemaphoreType.DMA((4, 8)),
                pltpu.SemaphoreType.DMA((4, 8)),
                pltpu.SemaphoreType.DMA((4,)),
            ],
            compiler_params=pltpu.CompilerParams(
                collective_id=0, has_side_effects=True, vmem_limit_bytes=62 * 1024 * 1024
            ),
        )(tracer, courant, displacement.transpose(0, 2, 3, 1), cotangent)

    in_specs = (
        P(None, "gy", "gx"),
        P(None, None, "gy", "gx"),
        P(None, None, "gy", "gx"),
        P(None, "gy", "gx"),
    )
    out_specs = (P(None, "gy", "gx"), P(None, None, "gy", "gx"))
    return jax.shard_map(body, mesh=mesh, in_specs=in_specs, out_specs=out_specs, check_vma=False)
```

```python
import jax
import jax.numpy as jnp
from jax import lax
from jax.experimental import pallas as pl
from jax.experimental.pallas import tpu as pltpu
from jax.sharding import PartitionSpec as P

NT = 6
SIDE = 128
HALO = 24
TALL = SIDE + 2 * HALO
WIN = SIDE + 8
PITCH = 21
WIDE = 18
PAD = 40
GROUP = 4
DEEP = 216
MESH = pl.DeviceIdType.MESH


def lagrange_weights(t):
    return (
        t * (t - 1.0) * (t - 2.0) * (-1.0 / 6.0),
        (t + 1.0) * (t - 1.0) * (t - 2.0) * 0.5,
        (t + 1.0) * t * (t - 2.0) * -0.5,
        (t + 1.0) * t * (t - 1.0) * (1.0 / 6.0),
    )


def lagrange_slopes(t):
    s = t * t
    return (
        (3.0 * s - 6.0 * t + 2.0) * (-1.0 / 6.0),
        (3.0 * s - 4.0 * t - 1.0) * 0.5,
        (3.0 * s - 2.0 * t - 2.0) * -0.5,
        (3.0 * s - 1.0) * (1.0 / 6.0),
    )


def kernel(
    sizes, tracer_in, courant_in, disp_in, cotangent_in, grad, sens,
    courant, disp, cotangent, q0, q1, s, c0, c1, w, lap, vp, eb, hb, f, fp, ma, rr, rc, rx, send, recv, load,
):
    nx, ny = sizes
    q, c = (q0, q1), (c0, c1)
    ix, iy = lax.axis_index("gx"), lax.axis_index("gy")
    left, right = lax.rem(ix + nx - 1, nx), lax.rem(ix + 1, nx)
    up, down = lax.rem(iy + ny - 1, ny), lax.rem(iy + 1, ny)

    loads = [
        pltpu.make_async_copy(src, dst, load.at[n])
        for n, (src, dst) in enumerate((
            (tracer_in, q0.at[:, pl.ds(HALO, SIDE)]),
            (disp_in, disp),
            (courant_in, courant),
            (cotangent_in, cotangent),
        ))
    ]
    for copy in loads:
        copy.start()

    barrier = pltpu.get_barrier_semaphore()
    around = (
        (left, iy), (right, iy), (ix, up), (ix, down),
        (left, up), (left, down), (right, up), (right, down),
    )
    for who in around:
        pl.semaphore_signal(barrier, inc=1, device_id=who, device_id_type=MESH)

    lane = lax.broadcasted_iota(jnp.int32, (8, SIDE), 1)
    top, main, low = pl.ds(0, HALO), pl.ds(HALO, SIDE), pl.ds(HALO + SIDE, HALO)
    first, last = pl.ds(0, HALO), pl.ds(SIDE - HALO, HALO)

    def rows(k, shift=0):
        return pl.ds((k * 8 if isinstance(k, int) else pl.multiple_of(k * 8, 8)) + shift, 8)

    def loop(count, block):
        def several(n, _):
            for j in range(GROUP):
                block(n * GROUP + j, 0)
            return 0

        if count >= 2 * GROUP:
            lax.fori_loop(0, count // GROUP, several, 0)
            rest = count - count % GROUP
        else:
            rest = 0
        for k in range(rest, count):
            block(k, 0)

    def make(stage, plan):
        return [
            pltpu.make_async_remote_copy(
                src_ref=src, dst_ref=dst,
                send_sem=send.at[stage, n], recv_sem=recv.at[stage, n],
                device_id=who, device_id_type=MESH,
            )
            for n, (src, dst, who) in enumerate(plan)
        ]

    def halo_copies(h):
        return make(h, (
            (s.at[h, 0], c[h].at[0, main], (left, iy)),
            (s.at[h, 1], c[h].at[1, main], (right, iy)),
            (s.at[h, 0, first], c[h].at[0, low], (left, up)),
            (s.at[h, 0, last], c[h].at[0, top], (left, down)),
            (s.at[h, 1, first], c[h].at[1, low], (right, up)),
            (s.at[h, 1, last], c[h].at[1, top], (right, down)),
            (q[h].at[:, pl.ds(HALO, HALO)], q[h].at[:, low], (ix, up)),
            (q[h].at[:, pl.ds(SIDE, HALO)], q[h].at[:, top], (ix, down)),
        ))

    def fold_copies(x):
        return make(2 + x, (
            (fp.at[x, 0, main], rc.at[x, 0], (right, iy)),
            (fp.at[x, 1, main], rc.at[x, 1], (left, iy)),
            (fp.at[x, 0, top], rx.at[x, 0, 0], (right, up)),
            (fp.at[x, 0, low], rx.at[x, 0, 1], (right, down)),
            (fp.at[x, 1, top], rx.at[x, 1, 0], (left, up)),
            (fp.at[x, 1, low], rx.at[x, 1, 1], (left, down)),
            (f.at[x, :, top], rr.at[x, 0], (ix, up)),
            (f.at[x, :, low], rr.at[x, 1], (ix, down)),
        ))

    right_lanes = [(lane >= PITCH * t) & (lane < PITCH * t + WIDE) for t in range(NT)]
    left_lanes = [
        (lane >= (PITCH * t - WIDE) % SIDE) & (lane < (PITCH * t - WIDE) % SIDE + WIDE)
        for t in range(NT)
    ]

    def turned(value, amount):
        return value if amount % SIDE == 0 else pltpu.roll(value, amount % SIDE, 1)

    def pack(values):
        near_low = jnp.zeros((8, SIDE), jnp.float32)
        near_high = near_low
        for t in range(NT):
            moved = turned(values[t], PITCH * t)
            near_low = jnp.where(right_lanes[t], moved, near_low)
            near_high = jnp.where(left_lanes[t], moved, near_high)
        return near_low, near_high

    def geometry(step):
        dy, dx = disp[step, 0, 0, 0], disp[step, 0, 0, 1]
        base = -2 - dx
        shifts = [base + b for b in range(4)]
        masks = [(lane >= v) & (lane < SIDE + v) for v in shifts]
        return dy, base, shifts, masks

    def fractions(step, k):
        return 1.0 - courant[step, 0, rows(k), :], 1.0 - courant[step, 1, rows(k), :]

    def make_windows(step):
        dy, base, shifts, masks = geometry(step)
        start = HALO - 2 - dy
        border = (lax.rem(lane, PITCH) < 3) & (lane < PITCH * NT)
        lim = jnp.where(border, -3, 0)
        take_low = lim <= base
        turns = [lax.rem(SIDE - v, SIDE) for v in shifts]

        def block(k, _):
            at = pl.ds(start + k * 8, 8)
            merged = jnp.where(take_low, c[step][0, at, :], c[step][1, at, :])
            for t in range(NT):
                side = turned(merged, -PITCH * t)
                mid = q[step][t, at, :]
                for b in range(4):
                    w[b, t, rows(k), :] = pltpu.roll(jnp.where(masks[b], mid, side), turns[b], 1)
            return 0

        loop(WIN // 8, block)

    def advect():
        def block(k, _):
            ty, tx = fractions(0, k)
            la, lb = lagrange_weights(ty), lagrange_weights(tx)
            done = []
            for t in range(NT):
                total = None
                for a in range(4):
                    line = lb[0] * w[0, t, rows(k, a), :]
                    for b in range(1, 4):
                        line = line + lb[b] * w[b, t, rows(k, a), :]
                    total = la[a] * line if total is None else total + la[a] * line
                q1[t, rows(k, HALO), :] = total
                done.append(total)
            s[1, 0, rows(k), :], s[1, 1, rows(k), :] = pack(done)
            return 0

        loop(SIDE // 8, block)

    def sensitivity(step, g):
        def block(k, _):
            ty, tx = fractions(step, k)
            la, lb = lagrange_weights(ty), lagrange_weights(tx)
            da, db = lagrange_slopes(ty), lagrange_slopes(tx)
            gs = [g[t, rows(k), :] for t in range(NT)]
            along_rows = along_cols = None
            for a in range(4):
                line = slope = None
                for b in range(4):
                    tap = gs[0] * w[b, 0, rows(k, a), :]
                    for t in range(1, NT):
                        tap = tap + gs[t] * w[b, t, rows(k, a), :]
                    line = lb[b] * tap if line is None else line + lb[b] * tap
                    slope = db[b] * tap if slope is None else slope + db[b] * tap
                along_rows = da[a] * line if along_rows is None else along_rows + da[a] * line
                along_cols = la[a] * slope if along_cols is None else along_cols + la[a] * slope
            sens[step, 0, rows(k), :] = -along_rows
            sens[step, 1, rows(k), :] = -along_cols
            return 0

        loop(SIDE // 8, block)

    def spread(step, g, x):
        dy, base, shifts, masks = geometry(step)
        turns = [lax.rem(SIDE + v, SIDE) for v in shifts]

        def weigh(k, _):
            ty, tx = fractions(step, k)
            la, lb = lagrange_weights(ty), lagrange_weights(tx)
            for a in range(4):
                lap[a, rows(k, 8), :] = la[a]
            for t in range(NT):
                value = g[t, rows(k), :]
                for b in range(4):
                    vp[b, t, rows(k, 8), :] = lb[b] * value
            return 0

        loop(SIDE // 8, weigh)

        def deposit(k, _):
            la = [lap[a, rows(k, 8 - a), :] for a in range(4)]
            rims = []
            for t in range(NT):
                mid = rim = jnp.zeros((8, SIDE), jnp.float32)
                for b in range(4):
                    total = la[0] * vp[b, t, rows(k, 8), :]
                    for a in range(1, 4):
                        total = total + la[a] * vp[b, t, rows(k, 8 - a), :]
                    moved = pltpu.roll(total, turns[b], 1)
                    mid = mid + jnp.where(masks[b], moved, 0.0)
                    rim = rim + jnp.where(masks[b], 0.0, moved)
                eb[t, rows(k, PAD), :] = mid
                rims.append(rim)
            hb[0, rows(k, PAD), :], hb[1, rows(k, PAD), :] = pack(rims)
            return 0

        loop(WIN // 8, deposit)
        start = PAD - HALO + 2 + dy

        def place(k, _):
            at = pl.ds(start + k * 8, 8)
            for t in range(NT):
                f[x, t, rows(k), :] = eb[t, at, :]
            for d in range(2):
                fp[x, d, rows(k), :] = hb[d, at, :]
            return 0

        loop(TALL // 8, place)

    def fold(x, out):
        for d in range(2):
            rc[x, d, last, :] += rx[x, d, 0]
            rc[x, d, first, :] += rx[x, d, 1]
        for t in range(NT):
            f[x, t, pl.ds(SIDE, HALO), :] += rr[x, 0, t]
            f[x, t, pl.ds(HALO, HALO), :] += rr[x, 1, t]

        def block(k, _):
            from_left, from_right = rc[x, 0, rows(k), :], rc[x, 1, rows(k), :]
            for t in range(NT):
                low_part = turned(jnp.where(right_lanes[t], from_left, 0.0), -PITCH * t)
                high_part = turned(jnp.where(left_lanes[t], from_right, 0.0), -PITCH * t)
                out[t, rows(k), :] = f[x, t, rows(k, HALO), :] + low_part + high_part
            return 0

        loop(SIDE // 8, block)

    def first_pack(k, _):
        values = [q0[t, rows(k, HALO), :] for t in range(NT)]
        s[0, 0, rows(k), :], s[0, 1, rows(k), :] = pack(values)
        return 0

    loads[0].wait()
    loop(SIDE // 8, first_pack)
    pl.semaphore_wait(barrier, 8)
    halo0 = halo_copies(0)
    for copy in halo0:
        copy.start()

    lap[:, 0:8, :] = jnp.zeros((4, 8, SIDE), jnp.float32)
    lap[:, SIDE + 8:, :] = jnp.zeros((4, 8, SIDE), jnp.float32)
    vp[:, :, 0:8, :] = jnp.zeros((4, NT, 8, SIDE), jnp.float32)
    vp[:, :, SIDE + 8:, :] = jnp.zeros((4, NT, 8, SIDE), jnp.float32)
    eb[:, 0:PAD, :] = jnp.zeros((NT, PAD, SIDE), jnp.float32)
    eb[:, PAD + WIN:, :] = jnp.zeros((NT, DEEP - PAD - WIN, SIDE), jnp.float32)
    hb[:, 0:PAD, :] = jnp.zeros((2, PAD, SIDE), jnp.float32)
    hb[:, PAD + WIN:, :] = jnp.zeros((2, DEEP - PAD - WIN, SIDE), jnp.float32)

    for copy in loads[1:]:
        copy.wait()
    spread(1, cotangent, 0)
    fold0 = fold_copies(0)
    for copy in fold0:
        copy.start()

    for copy in halo0:
        copy.wait_recv()
    make_windows(0)
    advect()
    halo1 = halo_copies(1)
    for copy in halo1:
        copy.start()

    for copy in fold0:
        copy.wait()
    fold(0, ma)
    spread(0, ma, 1)
    fold1 = fold_copies(1)
    for copy in fold1:
        copy.start()
    sensitivity(0, ma)

    for copy in halo1:
        copy.wait_recv()
    make_windows(1)
    sensitivity(1, cotangent)

    for copy in fold1:
        copy.wait()
    fold(1, grad)
    for copy in halo0 + halo1:
        copy.wait_send()


def solution(mesh):
    sizes = (mesh.shape["gx"], mesh.shape["gy"])
    f32 = jnp.float32

    def body(tracer, courant, displacement, cotangent):
        vmem = pl.BlockSpec(memory_space=pltpu.VMEM)
        return pl.pallas_call(
            lambda *refs: kernel(sizes, *refs),
            out_shape=(
                jax.ShapeDtypeStruct((NT, SIDE, SIDE), f32),
                jax.ShapeDtypeStruct((2, 2, SIDE, SIDE), f32),
            ),
            in_specs=[pl.BlockSpec(memory_space=pl.ANY)] * 4,
            out_specs=(vmem, vmem),
            scratch_shapes=[
                pltpu.VMEM((2, 2, SIDE, SIDE), f32),
                pltpu.SMEM((2, 1, 1, 2), jnp.int32),
                pltpu.VMEM((NT, SIDE, SIDE), f32),
                pltpu.VMEM((NT, TALL, SIDE), f32),
                pltpu.VMEM((NT, TALL, SIDE), f32),
                pltpu.VMEM((2, 2, SIDE, SIDE), f32),
                pltpu.VMEM((2, TALL, SIDE), f32),
                pltpu.VMEM((2, TALL, SIDE), f32),
                pltpu.VMEM((4, NT, WIN, SIDE), f32),
                pltpu.VMEM((4, SIDE + 16, SIDE), f32),
                pltpu.VMEM((4, NT, SIDE + 16, SIDE), f32),
                pltpu.VMEM((NT, DEEP, SIDE), f32),
                pltpu.VMEM((2, DEEP, SIDE), f32),
                pltpu.VMEM((2, NT, TALL, SIDE), f32),
                pltpu.VMEM((2, 2, TALL, SIDE), f32),
                pltpu.VMEM((NT, SIDE, SIDE), f32),
                pltpu.VMEM((2, 2, NT, HALO, SIDE), f32),
                pltpu.VMEM((2, 2, SIDE, SIDE), f32),
                pltpu.VMEM((2, 2, 2, HALO, SIDE), f32),
                pltpu.SemaphoreType.DMA((4, 8)),
                pltpu.SemaphoreType.DMA((4, 8)),
                pltpu.SemaphoreType.DMA((4,)),
            ],
            compiler_params=pltpu.CompilerParams(
                collective_id=0, has_side_effects=True, vmem_limit_bytes=62 * 1024 * 1024
            ),
        )(tracer, courant, displacement.transpose(0, 2, 3, 1), cotangent)

    in_specs = (
        P(None, "gy", "gx"),
        P(None, None, "gy", "gx"),
        P(None, None, "gy", "gx"),
        P(None, "gy", "gx"),
    )
    out_specs = (P(None, "gy", "gx"), P(None, None, "gy", "gx"))
    return jax.shard_map(body, mesh=mesh, in_specs=in_specs, out_specs=out_specs, check_vma=False)
```

```python
import jax
import jax.numpy as jnp
from jax import lax
from jax.experimental import pallas as pl
from jax.experimental.pallas import tpu as pltpu
from jax.sharding import PartitionSpec as P

NT = 6
SIDE = 128
HALO = 24
TALL = SIDE + 2 * HALO
WIN = SIDE + 8
PITCH = 21
WIDE = 18
PAD = 40
GROUP = 4
DEEP = 216
MESH = pl.DeviceIdType.MESH


def lagrange_weights(t):
    return (
        t * (t - 1.0) * (t - 2.0) * (-1.0 / 6.0),
        (t + 1.0) * (t - 1.0) * (t - 2.0) * 0.5,
        (t + 1.0) * t * (t - 2.0) * -0.5,
        (t + 1.0) * t * (t - 1.0) * (1.0 / 6.0),
    )


def lagrange_slopes(t):
    s = t * t
    return (
        (3.0 * s - 6.0 * t + 2.0) * (-1.0 / 6.0),
        (3.0 * s - 4.0 * t - 1.0) * 0.5,
        (3.0 * s - 2.0 * t - 2.0) * -0.5,
        (3.0 * s - 1.0) * (1.0 / 6.0),
    )


def kernel(
    sizes, tracer_in, courant_in, disp_in, cotangent_in, grad, sens,
    courant, disp, cotangent, q0, q1, s, c0, c1, w, lap, lbp, eb, hb, f, fp, ma, rr, rc, rx, send, recv, load,
):
    nx, ny = sizes
    q, c = (q0, q1), (c0, c1)
    ix, iy = lax.axis_index("gx"), lax.axis_index("gy")
    left, right = lax.rem(ix + nx - 1, nx), lax.rem(ix + 1, nx)
    up, down = lax.rem(iy + ny - 1, ny), lax.rem(iy + 1, ny)

    loads = [
        pltpu.make_async_copy(src, dst, load.at[n])
        for n, (src, dst) in enumerate((
            (tracer_in, q0.at[:, pl.ds(HALO, SIDE)]),
            (disp_in, disp),
            (courant_in, courant),
            (cotangent_in, cotangent.at[:, pl.ds(8, SIDE)]),
        ))
    ]
    for copy in loads:
        copy.start()

    barrier = pltpu.get_barrier_semaphore()
    around = (
        (left, iy), (right, iy), (ix, up), (ix, down),
        (left, up), (left, down), (right, up), (right, down),
    )
    for who in around:
        pl.semaphore_signal(barrier, inc=1, device_id=who, device_id_type=MESH)

    lane = lax.broadcasted_iota(jnp.int32, (8, SIDE), 1)
    top, main, low = pl.ds(0, HALO), pl.ds(HALO, SIDE), pl.ds(HALO + SIDE, HALO)
    first, last = pl.ds(0, HALO), pl.ds(SIDE - HALO, HALO)

    def rows(k, shift=0):
        return pl.ds((k * 8 if isinstance(k, int) else pl.multiple_of(k * 8, 8)) + shift, 8)

    def loop(count, block):
        def several(n, _):
            for j in range(GROUP):
                block(n * GROUP + j, 0)
            return 0

        if count >= 2 * GROUP:
            lax.fori_loop(0, count // GROUP, several, 0)
            rest = count - count % GROUP
        else:
            rest = 0
        for k in range(rest, count):
            block(k, 0)

    def make(stage, plan):
        return [
            pltpu.make_async_remote_copy(
                src_ref=src, dst_ref=dst,
                send_sem=send.at[stage, n], recv_sem=recv.at[stage, n],
                device_id=who, device_id_type=MESH,
            )
            for n, (src, dst, who) in enumerate(plan)
        ]

    def halo_copies(h):
        return make(h, (
            (s.at[h, 0], c[h].at[0, main], (left, iy)),
            (s.at[h, 1], c[h].at[1, main], (right, iy)),
            (s.at[h, 0, first], c[h].at[0, low], (left, up)),
            (s.at[h, 0, last], c[h].at[0, top], (left, down)),
            (s.at[h, 1, first], c[h].at[1, low], (right, up)),
            (s.at[h, 1, last], c[h].at[1, top], (right, down)),
            (q[h].at[:, pl.ds(HALO, HALO)], q[h].at[:, low], (ix, up)),
            (q[h].at[:, pl.ds(SIDE, HALO)], q[h].at[:, top], (ix, down)),
        ))

    def fold_copies(x):
        return make(2 + x, (
            (fp.at[x, 0, main], rc.at[x, 0], (right, iy)),
            (fp.at[x, 1, main], rc.at[x, 1], (left, iy)),
            (fp.at[x, 0, top], rx.at[x, 0, 0], (right, up)),
            (fp.at[x, 0, low], rx.at[x, 0, 1], (right, down)),
            (fp.at[x, 1, top], rx.at[x, 1, 0], (left, up)),
            (fp.at[x, 1, low], rx.at[x, 1, 1], (left, down)),
            (f.at[x, :, top], rr.at[x, 0], (ix, up)),
            (f.at[x, :, low], rr.at[x, 1], (ix, down)),
        ))

    right_lanes = [(lane >= PITCH * t) & (lane < PITCH * t + WIDE) for t in range(NT)]
    left_lanes = [
        (lane >= (PITCH * t - WIDE) % SIDE) & (lane < (PITCH * t - WIDE) % SIDE + WIDE)
        for t in range(NT)
    ]

    def turned(value, amount):
        return value if amount % SIDE == 0 else pltpu.roll(value, amount % SIDE, 1)

    def pack(values):
        near_low = jnp.zeros((8, SIDE), jnp.float32)
        near_high = near_low
        for t in range(NT):
            moved = turned(values[t], PITCH * t)
            near_low = jnp.where(right_lanes[t], moved, near_low)
            near_high = jnp.where(left_lanes[t], moved, near_high)
        return near_low, near_high

    def geometry(step):
        dy, dx = disp[step, 0, 0, 0], disp[step, 0, 0, 1]
        base = -2 - dx
        shifts = [base + b for b in range(4)]
        masks = [(lane >= v) & (lane < SIDE + v) for v in shifts]
        return dy, base, shifts, masks

    def fractions(step, k):
        return 1.0 - courant[step, 0, rows(k), :], 1.0 - courant[step, 1, rows(k), :]

    def make_windows(step):
        dy, base, shifts, masks = geometry(step)
        start = HALO - 2 - dy
        border = (lax.rem(lane, PITCH) < 3) & (lane < PITCH * NT)
        lim = jnp.where(border, -3, 0)
        take_low = lim <= base
        turns = [lax.rem(SIDE - v, SIDE) for v in shifts]

        def block(k, _):
            at = pl.ds(start + k * 8, 8)
            merged = jnp.where(take_low, c[step][0, at, :], c[step][1, at, :])
            for t in range(NT):
                side = turned(merged, -PITCH * t)
                mid = q[step][t, at, :]
                for b in range(4):
                    w[b, t, rows(k), :] = pltpu.roll(jnp.where(masks[b], mid, side), turns[b], 1)
            return 0

        loop(WIN // 8, block)

    def advect():
        def block(k, _):
            ty, tx = fractions(0, k)
            la, lb = lagrange_weights(ty), lagrange_weights(tx)
            done = []
            for t in range(NT):
                total = None
                for a in range(4):
                    line = lb[0] * w[0, t, rows(k, a), :]
                    for b in range(1, 4):
                        line = line + lb[b] * w[b, t, rows(k, a), :]
                    total = la[a] * line if total is None else total + la[a] * line
                q1[t, rows(k, HALO), :] = total
                done.append(total)
            s[1, 0, rows(k), :], s[1, 1, rows(k), :] = pack(done)
            return 0

        loop(SIDE // 8, block)

    def sensitivity(step, g):
        def block(k, _):
            ty, tx = fractions(step, k)
            la, lb = lagrange_weights(ty), lagrange_weights(tx)
            da, db = lagrange_slopes(ty), lagrange_slopes(tx)
            gs = [g[t, rows(k, 8), :] for t in range(NT)]
            along_rows = along_cols = None
            for a in range(4):
                line = slope = None
                for b in range(4):
                    tap = gs[0] * w[b, 0, rows(k, a), :]
                    for t in range(1, NT):
                        tap = tap + gs[t] * w[b, t, rows(k, a), :]
                    line = lb[b] * tap if line is None else line + lb[b] * tap
                    slope = db[b] * tap if slope is None else slope + db[b] * tap
                along_rows = da[a] * line if along_rows is None else along_rows + da[a] * line
                along_cols = la[a] * slope if along_cols is None else along_cols + la[a] * slope
            sens[step, 0, rows(k), :] = -along_rows
            sens[step, 1, rows(k), :] = -along_cols
            return 0

        loop(SIDE // 8, block)

    def spread(step, g, x):
        dy, base, shifts, masks = geometry(step)
        turns = [lax.rem(SIDE + v, SIDE) for v in shifts]

        def weigh(k, _):
            ty, tx = fractions(step, k)
            la, lb = lagrange_weights(ty), lagrange_weights(tx)
            for a in range(4):
                lap[a, rows(k, 8), :] = la[a]
                lbp[a, rows(k, 8), :] = lb[a]
            return 0

        loop(SIDE // 8, weigh)

        def deposit(k, _):
            factor = [
                [lap[a, rows(k, 8 - a), :] * lbp[b, rows(k, 8 - a), :] for a in range(4)]
                for b in range(4)
            ]
            rims = []
            for t in range(NT):
                values = [g[t, rows(k, 8 - a), :] for a in range(4)]
                mid = rim = jnp.zeros((8, SIDE), jnp.float32)
                for b in range(4):
                    total = factor[b][0] * values[0]
                    for a in range(1, 4):
                        total = total + factor[b][a] * values[a]
                    moved = pltpu.roll(total, turns[b], 1)
                    mid = mid + jnp.where(masks[b], moved, 0.0)
                    rim = rim + jnp.where(masks[b], 0.0, moved)
                eb[t, rows(k, PAD), :] = mid
                rims.append(rim)
            hb[0, rows(k, PAD), :], hb[1, rows(k, PAD), :] = pack(rims)
            return 0

        loop(WIN // 8, deposit)
        start = PAD - HALO + 2 + dy

        def place(k, _):
            at = pl.ds(start + k * 8, 8)
            for t in range(NT):
                f[x, t, rows(k), :] = eb[t, at, :]
            for d in range(2):
                fp[x, d, rows(k), :] = hb[d, at, :]
            return 0

        loop(TALL // 8, place)

    def fold(x, out, shift):
        for d in range(2):
            rc[x, d, last, :] += rx[x, d, 0]
            rc[x, d, first, :] += rx[x, d, 1]
        for t in range(NT):
            f[x, t, pl.ds(SIDE, HALO), :] += rr[x, 0, t]
            f[x, t, pl.ds(HALO, HALO), :] += rr[x, 1, t]

        def block(k, _):
            from_left, from_right = rc[x, 0, rows(k), :], rc[x, 1, rows(k), :]
            for t in range(NT):
                low_part = turned(jnp.where(right_lanes[t], from_left, 0.0), -PITCH * t)
                high_part = turned(jnp.where(left_lanes[t], from_right, 0.0), -PITCH * t)
                out[t, rows(k, shift), :] = f[x, t, rows(k, HALO), :] + low_part + high_part
            return 0

        loop(SIDE // 8, block)

    def first_pack(k, _):
        values = [q0[t, rows(k, HALO), :] for t in range(NT)]
        s[0, 0, rows(k), :], s[0, 1, rows(k), :] = pack(values)
        return 0

    loads[0].wait()
    loop(SIDE // 8, first_pack)
    pl.semaphore_wait(barrier, 8)
    halo0 = halo_copies(0)
    for copy in halo0:
        copy.start()

    lap[:, 0:8, :] = jnp.zeros((4, 8, SIDE), jnp.float32)
    lap[:, SIDE + 8:, :] = jnp.zeros((4, 8, SIDE), jnp.float32)
    lbp[:, 0:8, :] = jnp.zeros((4, 8, SIDE), jnp.float32)
    lbp[:, SIDE + 8:, :] = jnp.zeros((4, 8, SIDE), jnp.float32)
    for g in (cotangent, ma):
        g[:, 0:8, :] = jnp.zeros((NT, 8, SIDE), jnp.float32)
        g[:, SIDE + 8:, :] = jnp.zeros((NT, 8, SIDE), jnp.float32)
    eb[:, 0:PAD, :] = jnp.zeros((NT, PAD, SIDE), jnp.float32)
    eb[:, PAD + WIN:, :] = jnp.zeros((NT, DEEP - PAD - WIN, SIDE), jnp.float32)
    hb[:, 0:PAD, :] = jnp.zeros((2, PAD, SIDE), jnp.float32)
    hb[:, PAD + WIN:, :] = jnp.zeros((2, DEEP - PAD - WIN, SIDE), jnp.float32)

    for copy in loads[1:]:
        copy.wait()
    spread(1, cotangent, 0)
    fold0 = fold_copies(0)
    for copy in fold0:
        copy.start()

    for copy in halo0:
        copy.wait_recv()
    make_windows(0)
    advect()
    halo1 = halo_copies(1)
    for copy in halo1:
        copy.start()

    for copy in fold0:
        copy.wait()
    fold(0, ma, 8)
    spread(0, ma, 1)
    fold1 = fold_copies(1)
    for copy in fold1:
        copy.start()
    sensitivity(0, ma)

    for copy in halo1:
        copy.wait_recv()
    make_windows(1)
    sensitivity(1, cotangent)

    for copy in fold1:
        copy.wait()
    fold(1, grad, 0)
    for copy in halo0 + halo1:
        copy.wait_send()


def solution(mesh):
    sizes = (mesh.shape["gx"], mesh.shape["gy"])
    f32 = jnp.float32

    def body(tracer, courant, displacement, cotangent):
        vmem = pl.BlockSpec(memory_space=pltpu.VMEM)
        return pl.pallas_call(
            lambda *refs: kernel(sizes, *refs),
            out_shape=(
                jax.ShapeDtypeStruct((NT, SIDE, SIDE), f32),
                jax.ShapeDtypeStruct((2, 2, SIDE, SIDE), f32),
            ),
            in_specs=[pl.BlockSpec(memory_space=pl.ANY)] * 4,
            out_specs=(vmem, vmem),
            scratch_shapes=[
                pltpu.VMEM((2, 2, SIDE, SIDE), f32),
                pltpu.SMEM((2, 1, 1, 2), jnp.int32),
                pltpu.VMEM((NT, SIDE + 16, SIDE), f32),
                pltpu.VMEM((NT, TALL, SIDE), f32),
                pltpu.VMEM((NT, TALL, SIDE), f32),
                pltpu.VMEM((2, 2, SIDE, SIDE), f32),
                pltpu.VMEM((2, TALL, SIDE), f32),
                pltpu.VMEM((2, TALL, SIDE), f32),
                pltpu.VMEM((4, NT, WIN, SIDE), f32),
                pltpu.VMEM((4, SIDE + 16, SIDE), f32),
                pltpu.VMEM((4, SIDE + 16, SIDE), f32),
                pltpu.VMEM((NT, DEEP, SIDE), f32),
                pltpu.VMEM((2, DEEP, SIDE), f32),
                pltpu.VMEM((2, NT, TALL, SIDE), f32),
                pltpu.VMEM((2, 2, TALL, SIDE), f32),
                pltpu.VMEM((NT, SIDE + 16, SIDE), f32),
                pltpu.VMEM((2, 2, NT, HALO, SIDE), f32),
                pltpu.VMEM((2, 2, SIDE, SIDE), f32),
                pltpu.VMEM((2, 2, 2, HALO, SIDE), f32),
                pltpu.SemaphoreType.DMA((4, 8)),
                pltpu.SemaphoreType.DMA((4, 8)),
                pltpu.SemaphoreType.DMA((4,)),
            ],
            compiler_params=pltpu.CompilerParams(
                collective_id=0, has_side_effects=True, vmem_limit_bytes=62 * 1024 * 1024
            ),
        )(tracer, courant, displacement.transpose(0, 2, 3, 1), cotangent)

    in_specs = (
        P(None, "gy", "gx"),
        P(None, None, "gy", "gx"),
        P(None, None, "gy", "gx"),
        P(None, "gy", "gx"),
    )
    out_specs = (P(None, "gy", "gx"), P(None, None, "gy", "gx"))
    return jax.shard_map(body, mesh=mesh, in_specs=in_specs, out_specs=out_specs, check_vma=False)
```
